768 devices in a mesh: ab: 64 (over y, x, z_hi), cd: 12 (over z_lo, core).
Axes of the slice: x: 4, y: 8, z: 12 (z_hi: 2, z_lo: 6; z = z_hi * 6 + z_lo), core: 2. Of those that a mesh axis runs over, the one named last changes fastest.
Arguments:
- integrals: bfloat16 [32768, 12, 1024], P('ab', 'cd'), may hold values from -0.15625 to 0.15625
- amplitudes: bfloat16 [12, 1024, 3072], P('cd', 'ab'), may hold values from -6 to 6
- cd_irrep: int32 [12, 1024], P('cd', 'ab'), may hold values from 0 to 7, as said below
- residual: bfloat16 [32768, 3072], P('ab', 'cd'), may hold values from -6 to 6
- ab_energy: float32 [32768], P('ab'), may hold values from 1 to 4
- ij_energy: float32 [3072], P('cd'), may hold values from -2 to -0.5
Outputs:
- updated: bfloat16 [32768, 3072], P('ab', 'cd')
The draws below stay inside these ranges and needn't reach their ends.
Inputs may be any that keep to these rules, and one draw needn't show every extreme that they name: `cd_irrep`: values 0 to 7. In each aligned piece of 16 pairs of a slab at most 4 pairs have label 0, and every piece has at least one. In at least half of the slabs (rounded up) every piece has exactly 4.
All inputs are finite; a program needn't handle non-finite values.
Results may differ from the reference program's by a relative error of at most 0.018.
Values may be sent and summed in bfloat16 or wider, within the bound.
A program may use at most 32 MiB of HBM per device.

```python
import math
import jax
import jax.numpy as jnp
from jax import lax

CD_DEV = 1024
SLABS = 12
AB = 32768
IJ = 3072
PIECE = 16
LIVE = 4
N_AB = 64
N_CD = 12


def draw_cd_irrep(key, part):
    key = jax.random.fold_in(key, 11)
    first, second, third, fourth, fifth = jax.random.split(key, 5)
    counts = jax.random.randint(first, (SLABS, N_AB), 1, LIVE + 1)
    forced = jax.random.randint(second, (SLABS,), 0, N_AB)
    column = jnp.arange(N_AB, dtype=jnp.int32)[None, :]
    counts = jnp.where(column == forced[:, None], LIVE, counts)
    slab_order = jax.random.permutation(fifth, SLABS)
    full_slab = slab_order < (SLABS + 1) // 2
    counts = jnp.where(full_slab[:, None], LIVE, counts)
    scores = jax.random.randint(third, (SLABS, N_AB, PIECE), 0, 1 << 16) * PIECE + jnp.arange(PIECE, dtype=jnp.int32)
    ranks = jnp.argsort(jnp.argsort(scores, axis=-1), axis=-1)
    others = jax.random.randint(fourth, (SLABS, N_AB, PIECE), 1, 8)
    labels = jnp.where(ranks < counts[:, :, None], 0, others)
    return labels.reshape(SLABS, CD_DEV).astype(jnp.int32)


def level_of(stream_key, dims, pieces, low, largest):
    loudness, own = 1.0, jax.random.fold_in(stream_key, 6)
    for axis_at, shards_of in pieces:
        steps = jnp.exp(jax.random.uniform(jax.random.fold_in(own, axis_at), (shards_of,), jnp.float32, low / len(pieces), largest / len(pieces)))
        loudness = loudness * jnp.repeat(steps, dims[axis_at] // shards_of).reshape([-1 if axis == axis_at else 1 for axis in range(len(dims))])
    return loudness


def centred(own_key, shape, scale, most, shards=(), kind=jnp.bfloat16):
    gain = level_of(own_key, shape, shards, -0.22, 0.18) if shards else 1.0
    result = jax.random.normal(own_key, shape, jnp.float32) * scale * gain
    return jnp.minimum(jnp.maximum(result, -most), most).astype(kind)


def setup_inputs(seed: int = 0) -> dict:
    streams_of = jax.random.split(jax.random.key(seed), 7)
    return {
        "integrals": centred(streams_of[0], (AB, SLABS, CD_DEV), (N_CD * CD_DEV // 8) ** -0.5, 0.15625, ((0, 64), (1, 12))),
        "amplitudes": centred(streams_of[1], (SLABS, CD_DEV, IJ), 1.0, 6.0, ((0, 12), (1, 64))),
        "cd_irrep": draw_cd_irrep(jax.random.fold_in(streams_of[6], 71), 0),
        "residual": centred(streams_of[3], (AB, IJ), 1.0, 6.0, ((0, 64), (1, 12))),
        "ab_energy": jnp.clip(jnp.exp(math.log(4.0) - 1.3862944 * jax.random.uniform(streams_of[4], (AB,), jnp.float32) ** level_of(streams_of[4], (AB,), ((0, 64),), -0.2, 0.2)), 1.0, 4.0),
        "ij_energy": jnp.clip(-2.0 + 1.5 * jax.random.uniform(streams_of[5], (IJ,), jnp.float32) ** level_of(streams_of[5], (IJ,), ((0, 12),), -0.2, 0.2), -2.0, -0.5),
    }


def reference(integrals, amplitudes, cd_irrep, residual, ab_energy, ij_energy):
    keep = amplitudes * (cd_irrep == 0).astype(jnp.bfloat16)[:, :, None]

    def add_slab(slab, total):
        block = lax.dynamic_index_in_dim(integrals, slab, 1, keepdims=False)
        rows = lax.dynamic_index_in_dim(keep, slab, 0, keepdims=False)
        partial_sum = jnp.dot(block, rows, preferred_element_type=jnp.float32).astype(jnp.bfloat16)
        partial_sum = lax.optimization_barrier(partial_sum)
        return total + partial_sum.astype(jnp.float32)

    ladder = lax.fori_loop(0, SLABS, add_slab, jnp.zeros((AB, IJ), jnp.float32))
    denominator = ab_energy[:, None] - ij_energy[None, :]
    return ((residual.astype(jnp.float32) + ladder) / denominator).astype(jnp.bfloat16)
```

```python
import jax
import jax.numpy as jnp
from jax import lax
from jax.experimental import pallas as pl
from jax.experimental.pallas import tpu as pltpu
from jax.sharding import PartitionSpec as P

MESH = pl.DeviceIdType.MESH
NX, NY, NZ = 4, 8, 6
F32, BF16 = jnp.float32, jnp.bfloat16


def iota(shape, dim):
    return lax.broadcasted_iota(jnp.int32, shape, dim)


def kernel(
    v_hbm, t_hbm, lab_hbm, res_hbm, ab_hbm, ij_hbm,
    out_ref,
    lab, t_in, v_in, res, abe, ije, den,
    lx, ly, lz, tsend, tx, ty, vb, acc, xs, xr,
    loc, lxs, lxr, lys, lyr, lzs, tzs, tzr, txs, txr, tys, tyr, vs, vr, cs, late_in,
):
    ab, cd = lax.axis_index("ab"), lax.axis_index("cd")
    y, x, zh = ab // 8, (ab // 2) % 4, ab % 2
    zl, c = cd // 2, cd % 2

    def dev(yy=y, xx=x, hh=zh, ll=zl, cc=c):
        return ((yy * NX + xx) * 2 + hh, ll * 2 + cc)

    def rc(src, dst, ss, rs, to):
        return pltpu.make_async_remote_copy(
            src_ref=src, dst_ref=dst, send_sem=ss, recv_sem=rs, device_id=to, device_id_type=MESH
        )

    def xat(d):
        return lax.rem(x + d + NX, NX)

    def yat(d):
        return lax.rem(y + d + NY, NY)

    loads = [
        pltpu.make_async_copy(a, b, loc.at[i])
        for i, (a, b) in enumerate(
            [(lab_hbm, lab), (t_hbm, t_in), (v_hbm, v_in), (res_hbm, res), (ab_hbm, abe), (ij_hbm, ije)]
        )
    ]
    for cp in loads:
        cp.start()

    barrier = pltpu.get_barrier_semaphore()

    def hello(to):
        pl.semaphore_signal(barrier, inc=1, device_id=to, device_id_type=MESH)

    for d in range(1, NX):
        hello(dev(xx=xat(d)))
    for d in range(1, NY):
        hello(dev(yy=yat(d)))
    for d in range(1, NZ):
        hello(dev(ll=lax.rem(zl + d, NZ)))
    hello(dev(cc=1 - c))

    @pl.when(zh == 0)
    def _():
        for j in range(NZ):
            hello(dev(hh=1, ll=j))

    loads[0].wait()
    codes, count = [], jnp.int32(0)
    for p in range(16):
        live = jnp.where(lab[0, p] == 0, jnp.int32(1), jnp.int32(0))
        count = count + live
        codes.append(count * live)
    lane = iota((8, 128), 1)
    base = x * 32 + zh * 16
    mine = jnp.zeros((8, 128), F32)
    for p in range(16):
        mine = mine + jnp.where(lane == base + p, codes[p], 0).astype(F32)
    lx[0] = mine
    row, col = iota((16, 64), 0), iota((16, 64), 1)
    code_of = jnp.zeros((16, 64), jnp.int32)
    for p in range(16):
        code_of = code_of + jnp.where(col % 16 == p, codes[p], 0)
    pick = jnp.where((code_of > 0) & (row == (col // 16) * 4 + code_of - 1), 1.0, 0.0).astype(BF16)
    loads[1].wait()
    stacked = jnp.concatenate(
        [
            jnp.concatenate([t_in[:, j * 512 + g * 128 : j * 512 + g * 128 + 128] for j in range(NZ)], axis=1)
            for g in range(4)
        ],
        axis=0,
    )
    tiles = jnp.dot(pick, stacked, preferred_element_type=F32).astype(BF16)
    for j in range(NZ):
        tsend[j] = tiles[:, j * 128 : (j + 1) * 128]
    tx[0, x, zl] = tsend[zl]

    pl.semaphore_wait(barrier, jnp.where(zh == 0, 16, 22))

    @pl.when(zh == 1)
    def _():
        for j in range(NZ):
            pl.semaphore_signal(late_in, inc=1, device_id=dev(hh=0, ll=j), device_id_type=MESH)

    def label_x(d):
        return rc(lx.at[0], lx.at[d], lxs.at[d - 1], lxr.at[d - 1], dev(xx=xat(d)))

    for d in range(1, NX):
        label_x(d).start()

    def tile_near(j):
        return rc(tsend.at[j], tx.at[0, x, zl], tzs.at[0, j], tzr.at[0, zl], dev(ll=j))

    def tile_far(j):
        return rc(tsend.at[j], tx.at[1, x, zl], tzs.at[1, j], tzr.at[1, zl], dev(hh=1 - zh, ll=j))

    for j in range(NZ):

        @pl.when(zl != j)
        def _():
            tile_near(j).start()

    @pl.when(zh == 1)
    def _():
        for j in range(NZ):
            tile_far(j).start()

    for d in range(1, NX):
        label_x(d).wait_recv()
    ly[0] = (lx[0] + lx[1]) + (lx[2] + lx[3])

    def label_y(d):
        return rc(ly.at[0], ly.at[d], lys.at[d - 1], lyr.at[d - 1], dev(yy=yat(d)))

    for d in range(1, NY):
        label_y(d).start()

    def tile_wait(hi, j):
        rc(tsend.at[j], tx.at[hi, x, j], tzs.at[hi, j], tzr.at[hi, j], dev(ll=j)).wait_recv()

    def t_x(hi, d):
        return rc(tx.at[hi, x], tx.at[hi, x], txs.at[hi, d - 1], txr.at[hi, d - 1], dev(xx=xat(d)))

    def t_x_wait(hi, d):
        xo = xat(-d)
        rc(tx.at[hi, xo], tx.at[hi, xo], txs.at[hi, d - 1], txr.at[hi, d - 1], dev(xx=xo)).wait_recv()

    for j in range(NZ):

        @pl.when(zl != j)
        def _():
            tile_wait(0, j)

    for d in range(1, NX):
        t_x(0, d).start()

    for d in range(1, NY):
        label_y(d).wait_recv()
    rows8 = iota((8, 128), 0)
    plane = jnp.where(rows8 == y, ly[0], 0.0)
    for d in range(1, NY):
        plane = plane + jnp.where(rows8 == yat(-d), ly[d], 0.0)
    lz[0] = plane

    def compact(hi):
        ri, li = iota((16, 128), 0), iota((16, 128), 1)
        want = jnp.where(li // 32 == ri // 4, ri % 4 + 1, -1).astype(F32)
        parts = []
        for q in range(NY):
            block = jnp.where(jnp.broadcast_to(lz[hi, q : q + 1, :], (16, 128)) == want, 1.0, 0.0).astype(BF16)
            pieces = [block]
            if q:
                pieces.insert(0, jnp.zeros((16 * q, 128), BF16))
            if q < NY - 1:
                pieces.append(jnp.zeros((16 * (NY - 1 - q), 128), BF16))
            parts.append(jnp.concatenate(pieces, axis=0))
        select = jnp.concatenate(parts, axis=1)
        for sub in range(2):
            kept = lax.dot_general(
                v_in[sub * 256 : (sub + 1) * 256, :], select, (((1,), (1,)), ((), ())), preferred_element_type=F32
            )
            vb[zl, hi, sub] = kept.astype(BF16)
            v_send(0, hi, sub)

    def v_copy(way, k, hi, sub):
        slab = zl - k if way == 0 else zl + k
        here = vb.at[slab, hi, sub]
        return rc(
            here, here, vs.at[way, k, hi, sub], vr.at[way, k, hi, sub], dev(ll=zl + 1 if way == 0 else zl - 1)
        )

    def v_goes(way, k):
        return (zl >= k) & (zl < NZ - 1) if way == 0 else (zl + k < NZ) & (zl > 0)

    def v_send(k, hi, sub):
        for way in range(2):

            @pl.when(v_goes(way, k))
            def _():
                v_copy(way, k, hi, sub).start()

    def v_step(k, hi):
        for sub in range(2):
            for way in range(2):
                comes = zl >= k if way == 0 else zl + k < NZ

                @pl.when(comes)
                def _():
                    slab = zl - k if way == 0 else zl + k
                    here = vb.at[slab, hi, sub]
                    rc(
                        here, here, vs.at[way, k - 1, hi, sub], vr.at[way, k - 1, hi, sub],
                        dev(ll=zl - 1 if way == 0 else zl + 1),
                    ).wait_recv()

                if k < NZ - 1:

                    @pl.when(v_goes(way, k))
                    def _():
                        v_copy(way, k, hi, sub).start()

    def relayout(hi):
        i, j = iota((64, 64), 0), iota((64, 64), 1)
        perm = jnp.where(
            (i // 16 == (j // 4) % 4) & ((i // 4) % 4 == j // 16) & (i % 4 == j % 4), 1.0, 0.0
        ).astype(BF16)
        got = jnp.concatenate(
            [jnp.concatenate([tx[hi, xx, s] for xx in range(NX)], axis=0) for s in range(NZ)], axis=1
        )
        moved = jnp.dot(perm, got, preferred_element_type=F32).astype(BF16)
        for s in range(NZ):
            for g in range(4):
                ty[hi, y, s, :, g * 128 : (g + 1) * 128] = moved[g * 16 : (g + 1) * 16, s * 128 : (s + 1) * 128]

    def t_copy(hi, way, d, sub):
        here = ty.at[hi, yat(-d if way == 0 else d), pl.ds(3 * sub, 3)]
        return rc(here, here, tys.at[hi, way, d, sub], tyr.at[hi, way, d, sub], dev(yy=yat(1 if way == 0 else -1)))

    def t_goes(d, way, sub):
        return d < 3 or (d == 3 and sub == way)

    def t_step(hi, d):
        for sub in range(2):
            for way in range(2):
                if d > 0 and t_goes(d - 1, way, sub):
                    here = ty.at[hi, yat(-d if way == 0 else d), pl.ds(3 * sub, 3)]
                    rc(
                        here, here, tys.at[hi, way, d - 1, sub], tyr.at[hi, way, d - 1, sub],
                        dev(yy=yat(-1 if way == 0 else 1)),
                    ).wait_recv()
                if t_goes(d, way, sub):
                    t_copy(hi, way, d, sub).start()

    def multiply(s, first=False):
        right = jnp.concatenate([ty[hi, :, s].reshape(128, 512) for hi in range(2)], axis=0)
        for sub in range(2):
            left = jnp.concatenate([vb[s, 0, sub], vb[s, 1, sub]], axis=1)
            part = jnp.dot(left, right, preferred_element_type=F32)
            here = pl.ds(sub * 256, 256)
            acc[here, :] = part if first else acc[here, :] + part

    def multiply_at(k):
        @pl.when(zl >= k)
        def _():
            multiply(zl - k)

        @pl.when(zl + k < NZ)
        def _():
            multiply(zl + k)

    loads[2].wait()
    compact(0)
    v_step(1, 0)

    @pl.when(zh == 0)
    def _():
        pl.semaphore_wait(late_in, NZ)
        for j in range(NZ):
            tile_far(j).start()

    label_z = rc(lz.at[0], lz.at[1], lzs.at[0], lzs.at[1], dev(hh=1 - zh))
    label_z.start()

    for d in range(1, NX):
        t_x_wait(0, d)
    relayout(0)
    t_step(0, 0)
    v_step(2, 0)
    t_step(0, 1)
    for j in range(NZ):
        tile_wait(1, j)
    for d in range(1, NX):
        t_x(1, d).start()
    v_step(3, 0)
    t_step(0, 2)
    for d in range(1, NX):
        t_x_wait(1, d)
    relayout(1)
    t_step(1, 0)
    label_z.wait_recv()
    compact(1)
    v_step(4, 0)
    t_step(0, 3)
    t_step(1, 1)
    v_step(5, 0)
    t_step(0, 4)
    t_step(1, 2)
    v_step(1, 1)
    t_step(1, 3)
    v_step(2, 1)
    t_step(1, 4)

    loads[3].wait()
    loads[4].wait()
    loads[5].wait()
    for q in range(4):
        column = jnp.broadcast_to(abe[0:1, q * 128 : (q + 1) * 128], (128, 128)).T
        den[q * 128 : (q + 1) * 128, :] = jnp.concatenate([column, column], axis=1) - ije[...]
    multiply(zl, first=True)

    @pl.loop(1, 3)
    def _(k):
        multiply_at(k)

    for k in range(3, NZ):
        v_step(k, 1)

        @pl.loop(k, k + 1)
        def _(kk):
            multiply_at(kk)

    lo, hi_half = acc[:, :256], acc[:, 256:]
    xs[...] = jnp.where(c == 0, hi_half, lo).astype(BF16)
    swap = rc(xs, xr, cs.at[0], cs.at[1], dev(cc=1 - c))
    swap.start()
    own = jnp.where(c == 0, lo, hi_half) + res[...].astype(F32)
    swap.wait_recv()
    out_ref[...] = ((own + xr[...].astype(F32)) / den[...]).astype(BF16)

    swap.wait_send()
    label_z.wait_send()
    for d in range(1, NX):
        label_x(d).wait_send()
        t_x(0, d).wait_send()
        t_x(1, d).wait_send()
    for d in range(1, NY):
        label_y(d).wait_send()
    for j in range(NZ):

        @pl.when(zl != j)
        def _():
            tile_near(j).wait_send()

        tile_far(j).wait_send()
    for hi in range(2):
        for sub in range(2):
            for way in range(2):
                for d in range(4):
                    if t_goes(d, way, sub):
                        t_copy(hi, way, d, sub).wait_send()
                for k in range(NZ - 1):

                    @pl.when(v_goes(way, k))
                    def _():
                        v_copy(way, k, hi, sub).wait_send()


def local(integrals, amplitudes, cd_irrep, residual, ab_energy, ij_energy):
    anywhere = pl.BlockSpec(memory_space=pl.ANY)
    dma = pltpu.SemaphoreType.DMA
    return pl.pallas_call(
        kernel,
        out_shape=jax.ShapeDtypeStruct((512, 256), BF16),
        in_specs=[anywhere] * 6,
        out_specs=pl.BlockSpec(memory_space=pltpu.VMEM),
        scratch_shapes=[
            pltpu.SMEM((1, 16), jnp.int32),
            pltpu.VMEM((16, 3072), BF16),
            pltpu.VMEM((512, 1024), BF16),
            pltpu.VMEM((512, 256), BF16),
            pltpu.VMEM((1, 512), F32),
            pltpu.VMEM((1, 256), F32),
            pltpu.VMEM((512, 256), F32),
            pltpu.VMEM((NX, 8, 128), F32),
            pltpu.VMEM((NY, 8, 128), F32),
            pltpu.VMEM((2, 8, 128), F32),
            pltpu.VMEM((NZ, 16, 128), BF16),
            pltpu.VMEM((2, NX, NZ, 16, 128), BF16),
            pltpu.VMEM((2, NY, NZ, 16, 512), BF16),
            pltpu.VMEM((NZ, 2, 2, 256, 128), BF16),
            pltpu.VMEM((512, 512), F32),
            pltpu.VMEM((512, 256), BF16),
            pltpu.VMEM((512, 256), BF16),
            dma((6,)),
            dma((NX - 1,)),
            dma((NX - 1,)),
            dma((NY - 1,)),
            dma((NY - 1,)),
            dma((2,)),
            dma((2, NZ)),
            dma((2, NZ)),
            dma((2, NX - 1)),
            dma((2, NX - 1)),
            dma((2, 2, 4, 2)),
            dma((2, 2, 4, 2)),
            dma((2, NZ - 1, 2, 2)),
            dma((2, NZ - 1, 2, 2)),
            dma((2,)),
            pltpu.SemaphoreType.REGULAR,
        ],
        compiler_params=pltpu.CompilerParams(
            collective_id=0, has_side_effects=True, vmem_limit_bytes=56 * 1024 * 1024
        ),
        cost_estimate=pl.CostEstimate(flops=2 * 512 * 1536 * 512, bytes_accessed=2 << 20, transcendentals=0),
    )(
        integrals.reshape(512, 1024),
        amplitudes.reshape(16, 3072),
        cd_irrep,
        residual,
        ab_energy.reshape(1, 512),
        ij_energy.reshape(1, 256),
    )


def solution(mesh):
    return jax.shard_map(
        local,
        mesh=mesh,
        in_specs=(
            P("ab", "cd", None),
            P("cd", "ab", None),
            P("cd", "ab"),
            P("ab", "cd"),
            P("ab"),
            P("cd"),
        ),
        out_specs=P("ab", "cd"),
        check_vma=False,
    )
```

```python
import jax
import jax.numpy as jnp
from jax import lax
from jax.experimental import pallas as pl
from jax.experimental.pallas import tpu as pltpu
from jax.sharding import PartitionSpec as P

MESH = pl.DeviceIdType.MESH
NX, NY, NZ = 4, 8, 6
NS = 4
ROWS = 512 // NS
F32, BF16 = jnp.float32, jnp.bfloat16


def iota(shape, dim):
    return lax.broadcasted_iota(jnp.int32, shape, dim)


def kernel(
    v_hbm, t_hbm, lab_hbm, res_hbm, ab_hbm, ij_hbm,
    out_hbm,
    lab, t_in, v_in, res, abe, ije, den,
    lx, ly, tsend, tz, tb, vb, acc, xs, xr, out,
    loc, lxs, lxr, lfs, lys, lyr, tzs, tzr, tys, tyr, txs, txr, vs, vr, cs, outs, in_near, in_far,
):
    ab, cd = lax.axis_index("ab"), lax.axis_index("cd")
    y, x, zh = ab // 8, (ab // 2) % 4, ab % 2
    zl, c = cd // 2, cd % 2

    def dev(yy=y, xx=x, hh=zh, ll=zl, cc=c):
        return ((yy * NX + xx) * 2 + hh, ll * 2 + cc)

    def rc(src, dst, ss, rs, to):
        return pltpu.make_async_remote_copy(
            src_ref=src, dst_ref=dst, send_sem=ss, recv_sem=rs, device_id=to, device_id_type=MESH
        )

    def xat(d):
        return lax.rem(x + d + NX, NX)

    def yat(d):
        return lax.rem(y + d + NY, NY)

    loads = [
        pltpu.make_async_copy(a, b, loc.at[i])
        for i, (a, b) in enumerate(
            [(lab_hbm, lab), (t_hbm, t_in), (v_hbm, v_in), (res_hbm, res), (ab_hbm, abe), (ij_hbm, ije)]
        )
    ]
    for cp in loads:
        cp.start()

    barrier = pltpu.get_barrier_semaphore()

    def signal(sem, to):
        pl.semaphore_signal(sem, inc=1, device_id=to, device_id_type=MESH)

    for d in range(1, NX):
        signal(barrier, dev(xx=xat(d)))
    for d in range(1, NY):
        signal(barrier, dev(yy=yat(d)))
    signal(barrier, dev(cc=1 - c))

    @pl.when(zl > 0)
    def _():
        signal(barrier, dev(ll=zl - 1))

    for j in range(1, NZ):

        @pl.when(j > zl)
        def _():
            signal(barrier, dev(ll=j))

    def signal_other_half(sem):
        for j in range(NZ):
            signal(sem, dev(hh=1 - zh, ll=j))
        for d in range(1, NX):
            signal(sem, dev(hh=1 - zh, xx=xat(d)))

    @pl.when(zh == 0)
    def _():
        signal_other_half(barrier)

    loads[0].wait()
    codes, count = [], jnp.int32(0)
    for p in range(16):
        live = jnp.where(lab[0, p] == 0, jnp.int32(1), jnp.int32(0))
        count = count + live
        codes.append(count * live)
    lane = iota((1, 128), 1)
    base = x * 32 + zh * 16
    mine = jnp.zeros((1, 128), F32)
    for p in range(16):
        mine = mine + jnp.where(lane == base + p, codes[p], 0).astype(F32)
    lx[0, 0] = mine
    row, col = iota((16, 64), 0), iota((16, 64), 1)
    code_of = jnp.zeros((16, 64), jnp.int32)
    for p in range(16):
        code_of = code_of + jnp.where(col % 16 == p, codes[p], 0)
    pick = jnp.where((code_of > 0) & (row == (col // 16) * 4 + code_of - 1), 1.0, 0.0).astype(BF16)
    loads[1].wait()
    stacked = jnp.concatenate(
        [
            jnp.concatenate([t_in[:, j * 512 + g * 128 : j * 512 + g * 128 + 128] for j in range(NZ)], axis=1)
            for g in range(4)
        ],
        axis=0,
    )
    tiles = jnp.dot(pick, stacked, preferred_element_type=F32).astype(BF16)
    for j in range(NZ):
        tsend[j] = tiles[:, j * 128 : (j + 1) * 128]
    tz[0, y, zl] = tsend[zl]

    def label_x(d):
        return rc(lx.at[0, 0], lx.at[0, d], lxs.at[d - 1], lxr.at[0, d], dev(xx=xat(d)))

    def label_far(d):
        return rc(lx.at[0, 0], lx.at[1, d], lfs.at[d], lxr.at[1, d], dev(hh=1 - zh, xx=xat(d)))

    def label_y(hi, d):
        here = ly.at[hi, y]
        return rc(here, here, lys.at[hi, d - 1], lyr.at[hi, d - 1], dev(yy=yat(d)))

    def label_y_wait(hi, d):
        here = ly.at[hi, yat(-d)]
        rc(here, here, lys.at[hi, d - 1], lyr.at[hi, d - 1], dev(yy=yat(-d))).wait_recv()

    def tile_near(j):
        return rc(tsend.at[j], tz.at[0, y, zl], tzs.at[0, j], tzr.at[0, zl], dev(ll=j))

    def tile_far(j):
        return rc(tsend.at[j], tz.at[1, y, zl], tzs.at[1, j], tzr.at[1, zl], dev(hh=1 - zh, ll=j))

    def tile_wait(hi, j):
        rc(tsend.at[j], tz.at[hi, y, j], tzs.at[hi, j], tzr.at[hi, j], dev(ll=j)).wait_recv()

    def t_y(hi, d):
        here = tz.at[hi, y]
        return rc(here, here, tys.at[hi, d - 1], tyr.at[hi, d - 1], dev(yy=yat(d)))

    def t_y_wait(hi, d):
        here = tz.at[hi, yat(-d)]
        rc(here, here, tys.at[hi, d - 1], tyr.at[hi, d - 1], dev(yy=yat(-d))).wait_recv()

    def relayout(hi):
        i, j = iota((128, 128), 0), iota((128, 128), 1)
        perm = jnp.where(
            (i // 32 == (j // 4) % 4) & ((i // 4) % 8 == j // 16) & (i % 4 == j % 4), 1.0, 0.0
        ).astype(BF16)
        got = jnp.concatenate([tz[hi, :, s].reshape(128, 128) for s in range(NZ)], axis=1)
        moved = jnp.dot(perm, got, preferred_element_type=F32).astype(BF16)
        for s in range(NZ):
            for g in range(4):
                tb[hi, x, s, :, g * 128 : (g + 1) * 128] = moved[g * 32 : (g + 1) * 32, s * 128 : (s + 1) * 128]

    def t_x(hi, way, sub):
        here = tb.at[hi, x, pl.ds(3 * sub, 3)]
        return rc(here, here, txs.at[hi, way, sub], txr.at[hi, way, sub], dev(xx=xat(1 - 2 * way)))

    def t_x_wait(hi, way, sub):
        here = tb.at[hi, xat(2 * way - 1), pl.ds(3 * sub, 3)]
        rc(here, here, txs.at[hi, way, sub], txr.at[hi, way, sub], dev(xx=xat(2 * way - 1))).wait_recv()

    def t_x_on(hi, way):
        here = tb.at[hi, xat(2 * way - 1), pl.ds(3 * way, 3)]
        return rc(here, here, txs.at[hi, way, 2], txr.at[hi, way, 2], dev(xx=xat(1 - 2 * way)))

    def t_x_start(hi):
        for k in range(2):
            for way in range(2):
                t_x(hi, way, (way + k) % 2).start()

    def t_x_relay(hi):
        for way in range(2):
            t_x_wait(hi, way, way)
            t_x_on(hi, way).start()

    def t_x_end(hi):
        for way in range(2):
            t_x_wait(hi, way, 1 - way)
            here = tb.at[hi, xat(2), pl.ds(3 * way, 3)]
            rc(here, here, txs.at[hi, way, 2], txr.at[hi, way, 2], dev(xx=xat(2 * way - 1))).wait_recv()

    def v_out(way, k, hi, sub):
        here = vb.at[zl - k if way == 0 else zl + k, hi, sub]
        return rc(
            here, here, vs.at[way, k, hi, sub], vr.at[way, k, hi, sub], dev(ll=zl + 1 if way == 0 else zl - 1)
        )

    def v_goes(way, k):
        return (zl >= k) & (zl < NZ - 1) if way == 0 else (zl + k < NZ) & (zl > 0)

    def v_comes(way, k):
        return zl >= k if way == 0 else zl + k < NZ

    def v_arrive(k, hi, sub):
        for way in range(2):

            @pl.when(v_comes(way, k))
            def _():
                here = vb.at[zl - k if way == 0 else zl + k, hi, sub]
                rc(
                    here, here, vs.at[way, k - 1, hi, sub], vr.at[way, k - 1, hi, sub],
                    dev(ll=zl - 1 if way == 0 else zl + 1),
                ).wait_recv()

            if k < NZ - 1:

                @pl.when(v_goes(way, k))
                def _():
                    v_out(way, k, hi, sub).start()

    def v_step(k, hi):
        for sub in range(NS):
            v_arrive(k, hi, sub)

    def compact(hi):
        ri, li = iota((128, 128), 0), iota((128, 128), 1)
        want = jnp.where(li // 32 == ri // 32, ri % 4 + 1, -1)
        parts = []
        for q in range(NY):
            mark = jnp.where((ri // 4) % 8 == q, want, -1).astype(F32)
            parts.append(jnp.where(jnp.broadcast_to(ly[hi, q], (128, 128)) == mark, 1.0, 0.0).astype(BF16))
        select = jnp.concatenate(parts, axis=1)
        for sub in range(NS):
            kept = lax.dot_general(
                v_in[sub * ROWS : (sub + 1) * ROWS, :], select, (((1,), (1,)), ((), ())), preferred_element_type=F32
            )
            vb[zl, hi, sub] = kept.astype(BF16)
            for way in range(2):

                @pl.when(v_goes(way, 0))
                def _():
                    v_out(way, 0, hi, sub).start()

    def right_of(s, hi):
        return tb[hi, :, s].reshape(128, 512)

    def multiply(s, first=False):
        right = jnp.concatenate([right_of(s, 0), right_of(s, 1)], axis=0)
        for sub in range(NS):
            left = jnp.concatenate([vb[s, 0, sub], vb[s, 1, sub]], axis=1)
            part = jnp.dot(left, right, preferred_element_type=F32)
            here = pl.ds(sub * ROWS, ROWS)
            acc[here, :] = part if first else acc[here, :] + part

    def multiply_at(k):
        @pl.when(zl >= k)
        def _():
            multiply(zl - k)

        @pl.when(zl + k < NZ)
        def _():
            multiply(zl + k)

    far = jnp.where(zl == 0, NZ - 1, 0)

    def multiply_last(hi, sub):
        @pl.when((zl == 0) | (zl == NZ - 1))
        def _():
            here = pl.ds(sub * ROWS, ROWS)
            acc[here, :] += jnp.dot(vb[far, hi, sub], right_of(far, hi), preferred_element_type=F32)

    pl.semaphore_wait(barrier, 11 + zl + zh * 9 + jnp.where(zl < NZ - 1, 1, 0))
    for d in range(1, NX):
        label_x(d).start()

    @pl.when(zh == 1)
    def _():
        signal_other_half(in_far)
        for d in range(NX):
            label_far(d).start()
        for j in range(NZ):
            tile_far(j).start()

    for j in range(NZ - 1):

        @pl.when(zl > j)
        def _():
            signal(in_near, dev(ll=j))
            tile_near(j).start()

    for d in range(1, NX):
        label_x(d).wait_recv()
    ly[0, y] = (lx[0, 0] + lx[0, 1]) + (lx[0, 2] + lx[0, 3])
    for d in range(1, NY):
        label_y(0, d).start()
    for d in range(1, NY):
        label_y_wait(0, d)
    loads[2].wait()
    compact(0)

    @pl.when(zl < NZ - 1)
    def _():
        pl.semaphore_wait(in_near, NZ - 1 - zl)

    for j in range(1, NZ):

        @pl.when(zl < j)
        def _():
            tile_near(j).start()

    for j in range(NZ):

        @pl.when(zl != j)
        def _():
            tile_wait(0, j)

    for d in range(1, NY):
        t_y(0, d).start()
    v_step(1, 0)

    @pl.when(zh == 0)
    def _():
        pl.semaphore_wait(in_far, 9)
        for d in range(NX):
            label_far(d).start()
        for j in range(NZ):
            tile_far(j).start()

    for j in range(NZ):
        tile_wait(1, j)
    for d in range(1, NY):
        t_y(1, d).start()
    for d in range(NX):
        rc(lx.at[0, 0], lx.at[1, d], lfs.at[d], lxr.at[1, d], dev(hh=1 - zh, xx=xat(d))).wait_recv()
    ly[1, y] = (lx[1, 0] + lx[1, 1]) + (lx[1, 2] + lx[1, 3])
    for d in range(1, NY):
        label_y(1, d).start()
    v_step(2, 0)
    for d in range(1, NY):
        t_y_wait(0, d)
    relayout(0)
    t_x_start(0)
    for d in range(1, NY):
        label_y_wait(1, d)
    compact(1)
    v_step(3, 0)
    for d in range(1, NY):
        t_y_wait(1, d)
    relayout(1)
    t_x_start(1)
    v_step(1, 1)
    t_x_relay(0)
    v_step(4, 0)
    v_step(2, 1)
    t_x_relay(1)
    v_step(5, 0)
    t_x_end(0)
    v_step(3, 1)
    t_x_end(1)

    loads[3].wait()
    loads[4].wait()
    loads[5].wait()
    for q in range(4):
        column = jnp.broadcast_to(abe[0:1, q * 128 : (q + 1) * 128], (128, 128)).T
        den[q * 128 : (q + 1) * 128, :] = jnp.concatenate([column, column], axis=1) - ije[...]
    multiply(zl, first=True)

    @pl.loop(1, 4)
    def _(k):
        multiply_at(k)

    v_step(4, 1)

    @pl.loop(4, 5)
    def _(k):
        multiply_at(k)

    for sub in range(NS):
        multiply_last(0, sub)

    def swap(sub):
        here = pl.ds(sub * ROWS, ROWS)
        return rc(xs.at[here], xr.at[here], cs.at[0, sub], cs.at[1, sub], dev(cc=1 - c))

    def put(sub):
        here = pl.ds(sub * ROWS, ROWS)
        return pltpu.make_async_copy(out.at[here], out_hbm.at[here], outs.at[sub])

    for sub in range(NS):
        v_arrive(NZ - 1, 1, sub)
        multiply_last(1, sub)
        here = pl.ds(sub * ROWS, ROWS)
        xs[here, :] = jnp.where(c == 0, acc[here, 256:], acc[here, :256]).astype(BF16)
        swap(sub).start()
    for sub in range(NS):
        here = pl.ds(sub * ROWS, ROWS)
        own = jnp.where(c == 0, acc[here, :256], acc[here, 256:]) + res[here, :].astype(F32)
        swap(sub).wait_recv()
        out[here, :] = ((own + xr[here, :].astype(F32)) / den[here, :]).astype(BF16)
        put(sub).start()

    for d in range(1, NX):
        label_x(d).wait_send()
    for d in range(NX):
        label_far(d).wait_send()
    for j in range(NZ):

        @pl.when(zl != j)
        def _():
            tile_near(j).wait_send()

        tile_far(j).wait_send()
    for hi in range(2):
        for d in range(1, NY):
            label_y(hi, d).wait_send()
            t_y(hi, d).wait_send()
        for way in range(2):
            t_x(hi, way, 0).wait_send()
            t_x(hi, way, 1).wait_send()
            t_x_on(hi, way).wait_send()
        for sub in range(NS):
            for way in range(2):
                for k in range(NZ - 1):

                    @pl.when(v_goes(way, k))
                    def _():
                        v_out(way, k, hi, sub).wait_send()

    for sub in range(NS):
        swap(sub).wait_send()
        put(sub).wait()


def local(integrals, amplitudes, cd_irrep, residual, ab_energy, ij_energy):
    anywhere = pl.BlockSpec(memory_space=pl.ANY)
    dma = pltpu.SemaphoreType.DMA
    return pl.pallas_call(
        kernel,
        out_shape=jax.ShapeDtypeStruct((512, 256), BF16),
        in_specs=[anywhere] * 6,
        out_specs=anywhere,
        scratch_shapes=[
            pltpu.SMEM((1, 16), jnp.int32),
            pltpu.VMEM((16, 3072), BF16),
            pltpu.VMEM((512, 1024), BF16),
            pltpu.VMEM((512, 256), BF16),
            pltpu.VMEM((1, 512), F32),
            pltpu.VMEM((1, 256), F32),
            pltpu.VMEM((512, 256), F32),
            pltpu.VMEM((2, NX, 1, 128), F32),
            pltpu.VMEM((2, NY, 1, 128), F32),
            pltpu.VMEM((NZ, 16, 128), BF16),
            pltpu.VMEM((2, NY, NZ, 16, 128), BF16),
            pltpu.VMEM((2, NX, NZ, 32, 512), BF16),
            pltpu.VMEM((NZ, 2, NS, ROWS, 128), BF16),
            pltpu.VMEM((512, 512), F32),
            pltpu.VMEM((512, 256), BF16),
            pltpu.VMEM((512, 256), BF16),
            pltpu.VMEM((512, 256), BF16),
            dma((6,)),
            dma((NX - 1,)),
            dma((2, NX)),
            dma((NX,)),
            dma((2, NY - 1)),
            dma((2, NY - 1)),
            dma((2, NZ)),
            dma((2, NZ)),
            dma((2, NY - 1)),
            dma((2, NY - 1)),
            dma((2, 2, 3)),
            dma((2, 2, 3)),
            dma((2, NZ - 1, 2, NS)),
            dma((2, NZ - 1, 2, NS)),
            dma((2, NS)),
            dma((NS,)),
            pltpu.SemaphoreType.REGULAR,
            pltpu.SemaphoreType.REGULAR,
        ],
        compiler_params=pltpu.CompilerParams(
            collective_id=0, has_side_effects=True, vmem_limit_bytes=56 * 1024 * 1024
        ),
        cost_estimate=pl.CostEstimate(flops=2 * 512 * 1536 * 512, bytes_accessed=2 << 20, transcendentals=0),
    )(
        integrals.reshape(512, 1024),
        amplitudes.reshape(16, 3072),
        cd_irrep,
        residual,
        ab_energy.reshape(1, 512),
        ij_energy.reshape(1, 256),
    )


def solution(mesh):
    return jax.shard_map(
        local,
        mesh=mesh,
        in_specs=(
            P("ab", "cd", None),
            P("cd", "ab", None),
            P("cd", "ab"),
            P("ab", "cd"),
            P("ab"),
            P("cd"),
        ),
        out_specs=P("ab", "cd"),
        check_vma=False,
    )
```

```python
import jax
import jax.numpy as jnp
from jax import lax
from jax.experimental import pallas as pl
from jax.experimental.pallas import tpu as pltpu
from jax.sharding import PartitionSpec as P

MESH = pl.DeviceIdType.MESH
NX, NY, NZ = 4, 8, 6
NS = 4
ROWS = 512 // NS
F32, BF16 = jnp.float32, jnp.bfloat16


def iota(shape, dim):
    return lax.broadcasted_iota(jnp.int32, shape, dim)


def kernel(
    v_hbm, t_hbm, lab_hbm, res_hbm, ab_hbm, ij_hbm,
    out_hbm,
    lab, t_in, v_in, res, abe, ije, den,
    lx, ly, tsend, tz, tb, vb, acc, xs, xr, out,
    loc, lxs, lxr, lfs, lys, lyr, tzs, tzr, tys, tyr, txs, txr, vs, vr, cs, outs, in_near, in_far,
):
    ab, cd = lax.axis_index("ab"), lax.axis_index("cd")
    y, x, zh = ab // 8, (ab // 2) % 4, ab % 2
    zl, c = cd // 2, cd % 2

    def dev(yy=y, xx=x, hh=zh, ll=zl, cc=c):
        return ((yy * NX + xx) * 2 + hh, ll * 2 + cc)

    def rc(src, dst, ss, rs, to):
        return pltpu.make_async_remote_copy(
            src_ref=src, dst_ref=dst, send_sem=ss, recv_sem=rs, device_id=to, device_id_type=MESH
        )

    def xat(d):
        return lax.rem(x + d + NX, NX)

    def yat(d):
        return lax.rem(y + d + NY, NY)

    loads = [
        pltpu.make_async_copy(a, b, loc.at[i])
        for i, (a, b) in enumerate(
            [(lab_hbm, lab), (t_hbm, t_in), (v_hbm, v_in), (res_hbm, res), (ab_hbm, abe), (ij_hbm, ije)]
        )
    ]
    for cp in loads:
        cp.start()

    barrier = pltpu.get_barrier_semaphore()

    def signal(sem, to):
        pl.semaphore_signal(sem, inc=1, device_id=to, device_id_type=MESH)

    for d in range(1, NX):
        signal(barrier, dev(xx=xat(d)))
    for d in range(1, NY):
        signal(barrier, dev(yy=yat(d)))
    signal(barrier, dev(cc=1 - c))

    @pl.when(zl > 0)
    def _():
        signal(barrier, dev(ll=zl - 1))

    for j in range(1, NZ):

        @pl.when(j > zl)
        def _():
            signal(barrier, dev(ll=j))

    def signal_other_half(sem):
        for j in range(NZ):
            signal(sem, dev(hh=1 - zh, ll=j))
        for d in range(1, NX):
            signal(sem, dev(hh=1 - zh, xx=xat(d)))

    @pl.when(zh == 0)
    def _():
        signal_other_half(barrier)

    loads[0].wait()
    codes, count = [], jnp.int32(0)
    for p in range(16):
        live = jnp.where(lab[0, p] == 0, jnp.int32(1), jnp.int32(0))
        count = count + live
        codes.append(count * live)
    lane = iota((1, 128), 1)
    base = x * 32 + zh * 16
    mine = jnp.zeros((1, 128), F32)
    for p in range(16):
        mine = mine + jnp.where(lane == base + p, codes[p], 0).astype(F32)
    lx[0, 0] = mine
    row, col = iota((16, 64), 0), iota((16, 64), 1)
    code_of = jnp.zeros((16, 64), jnp.int32)
    for p in range(16):
        code_of = code_of + jnp.where(col % 16 == p, codes[p], 0)
    pick = jnp.where((code_of > 0) & (row == (col // 16) * 4 + code_of - 1), 1.0, 0.0).astype(BF16)
    loads[1].wait()
    stacked = jnp.concatenate(
        [
            jnp.concatenate([t_in[:, j * 512 + g * 128 : j * 512 + g * 128 + 128] for j in range(NZ)], axis=1)
            for g in range(4)
        ],
        axis=0,
    )
    tiles = jnp.dot(pick, stacked, preferred_element_type=F32).astype(BF16)
    for j in range(NZ):
        tsend[j] = tiles[:, j * 128 : (j + 1) * 128]
    tz[0, y, zl] = tsend[zl]

    def label_x(d):
        return rc(lx.at[0, 0], lx.at[0, d], lxs.at[d - 1], lxr.at[0, d], dev(xx=xat(d)))

    def label_far(d):
        return rc(lx.at[0, 0], lx.at[1, d], lfs.at[d], lxr.at[1, d], dev(hh=1 - zh, xx=xat(d)))

    def label_y(hi, d):
        here = ly.at[hi, y]
        return rc(here, here, lys.at[hi, d - 1], lyr.at[hi, d - 1], dev(yy=yat(d)))

    def label_y_wait(hi, d):
        here = ly.at[hi, yat(-d)]
        rc(here, here, lys.at[hi, d - 1], lyr.at[hi, d - 1], dev(yy=yat(-d))).wait_recv()

    def tile_near(j):
        return rc(tsend.at[j], tz.at[0, y, zl], tzs.at[0, j], tzr.at[0, zl], dev(ll=j))

    def tile_far(j):
        return rc(tsend.at[j], tz.at[1, y, zl], tzs.at[1, j], tzr.at[1, zl], dev(hh=1 - zh, ll=j))

    def tile_wait(hi, j):
        rc(tsend.at[j], tz.at[hi, y, j], tzs.at[hi, j], tzr.at[hi, j], dev(ll=j)).wait_recv()

    def t_y(hi, d):
        here = tz.at[hi, y]
        return rc(here, here, tys.at[hi, d - 1], tyr.at[hi, d - 1], dev(yy=yat(d)))

    def t_y_wait(hi, d):
        here = tz.at[hi, yat(-d)]
        rc(here, here, tys.at[hi, d - 1], tyr.at[hi, d - 1], dev(yy=yat(-d))).wait_recv()

    def relayout(hi):
        i, j = iota((128, 128), 0), iota((128, 128), 1)
        perm = jnp.where(
            (i // 32 == (j // 4) % 4) & ((i // 4) % 8 == j // 16) & (i % 4 == j % 4), 1.0, 0.0
        ).astype(BF16)
        got = jnp.concatenate([tz[hi, :, s].reshape(128, 128) for s in range(NZ)], axis=1)
        moved = jnp.dot(perm, got, preferred_element_type=F32).astype(BF16)
        for s in range(NZ):
            for g in range(4):
                tb[hi, x, s, :, g * 128 : (g + 1) * 128] = moved[g * 32 : (g + 1) * 32, s * 128 : (s + 1) * 128]

    def t_x(hi, way, sub):
        here = tb.at[hi, x, pl.ds(3 * sub, 3)]
        return rc(here, here, txs.at[hi, way, sub], txr.at[hi, way, sub], dev(xx=xat(1 - 2 * way)))

    def t_x_wait(hi, way, sub):
        here = tb.at[hi, xat(2 * way - 1), pl.ds(3 * sub, 3)]
        rc(here, here, txs.at[hi, way, sub], txr.at[hi, way, sub], dev(xx=xat(2 * way - 1))).wait_recv()

    def t_x_on(hi, way):
        here = tb.at[hi, xat(2 * way - 1), pl.ds(3 * way, 3)]
        return rc(here, here, txs.at[hi, way, 2], txr.at[hi, way, 2], dev(xx=xat(1 - 2 * way)))

    def t_x_start(hi):
        for k in range(2):
            for way in range(2):
                t_x(hi, way, (way + k) % 2).start()

    def t_x_relay(hi):
        for way in range(2):
            t_x_wait(hi, way, way)
            t_x_on(hi, way).start()

    def t_x_end(hi):
        for way in range(2):
            t_x_wait(hi, way, 1 - way)
            here = tb.at[hi, xat(2), pl.ds(3 * way, 3)]
            rc(here, here, txs.at[hi, way, 2], txr.at[hi, way, 2], dev(xx=xat(2 * way - 1))).wait_recv()

    def v_out(way, k, hi, sub):
        here = vb.at[zl - k if way == 0 else zl + k, hi, sub]
        return rc(
            here, here, vs.at[way, k, hi, sub], vr.at[way, k, hi, sub], dev(ll=zl + 1 if way == 0 else zl - 1)
        )

    def v_goes(way, k):
        return (zl >= k) & (zl < NZ - 1) if way == 0 else (zl + k < NZ) & (zl > 0)

    def v_comes(way, k):
        return zl >= k if way == 0 else zl + k < NZ

    def v_arrive(k, hi, sub):
        for way in range(2):

            @pl.when(v_comes(way, k))
            def _():
                here = vb.at[zl - k if way == 0 else zl + k, hi, sub]
                rc(
                    here, here, vs.at[way, k - 1, hi, sub], vr.at[way, k - 1, hi, sub],
                    dev(ll=zl - 1 if way == 0 else zl + 1),
                ).wait_recv()

            if k < NZ - 1:

                @pl.when(v_goes(way, k))
                def _():
                    v_out(way, k, hi, sub).start()

    def v_step(k, hi):
        for sub in range(NS):
            v_arrive(k, hi, sub)

    def compact(hi):
        ri, li = iota((128, 128), 0), iota((128, 128), 1)
        want = jnp.where(li // 32 == ri // 32, ri % 4 + 1, -1)
        parts = []
        for q in range(NY):
            mark = jnp.where((ri // 4) % 8 == q, want, -1).astype(F32)
            parts.append(jnp.where(jnp.broadcast_to(ly[hi, q], (128, 128)) == mark, 1.0, 0.0).astype(BF16))
        select = jnp.concatenate(parts, axis=1)
        for sub in range(NS):
            kept = lax.dot_general(
                v_in[sub * ROWS : (sub + 1) * ROWS, :], select, (((1,), (1,)), ((), ())), preferred_element_type=F32
            )
            vb[zl, hi, sub] = kept.astype(BF16)
            for way in range(2):

                @pl.when(v_goes(way, 0))
                def _():
                    v_out(way, 0, hi, sub).start()

    def right_of(s, hi):
        return tb[hi, :, s].reshape(128, 512)

    def multiply(s, first=False):
        right = jnp.concatenate([right_of(s, 0), right_of(s, 1)], axis=0)
        for sub in range(NS):
            left = jnp.concatenate([vb[s, 0, sub], vb[s, 1, sub]], axis=1)
            part = jnp.dot(left, right, preferred_element_type=F32)
            here = pl.ds(sub * ROWS, ROWS)
            acc[here, :] = part if first else acc[here, :] + part

    def multiply_at(k):
        @pl.when(zl >= k)
        def _():
            multiply(zl - k)

        @pl.when(zl + k < NZ)
        def _():
            multiply(zl + k)

    far = jnp.where(zl == 0, NZ - 1, 0)

    def multiply_last(hi, sub):
        @pl.when((zl == 0) | (zl == NZ - 1))
        def _():
            here = pl.ds(sub * ROWS, ROWS)
            acc[here, :] += jnp.dot(vb[far, hi, sub], right_of(far, hi), preferred_element_type=F32)

    pl.semaphore_wait(barrier, 11 + zl + zh * 9 + jnp.where(zl < NZ - 1, 1, 0))
    for d in range(1, NX):
        label_x(d).start()

    @pl.when(zh == 1)
    def _():
        signal_other_half(in_far)
        for d in range(NX):
            label_far(d).start()
        for j in range(NZ):
            tile_far(j).start()

    for j in range(NZ - 1):

        @pl.when(zl > j)
        def _():
            signal(in_near, dev(ll=j))
            tile_near(j).start()

    for d in range(1, NX):
        label_x(d).wait_recv()
    ly[0, y] = (lx[0, 0] + lx[0, 1]) + (lx[0, 2] + lx[0, 3])
    for d in range(1, NY):
        label_y(0, d).start()
    for d in range(1, NY):
        label_y_wait(0, d)
    loads[2].wait()
    compact(0)

    loads[3].wait()
    loads[4].wait()
    loads[5].wait()
    for q in range(4):
        column = jnp.broadcast_to(abe[0:1, q * 128 : (q + 1) * 128], (128, 128)).T
        den[q * 128 : (q + 1) * 128, :] = jnp.concatenate([column, column], axis=1) - ije[...]

    @pl.when(zl < NZ - 1)
    def _():
        pl.semaphore_wait(in_near, NZ - 1 - zl)

    for j in range(1, NZ):

        @pl.when(zl < j)
        def _():
            tile_near(j).start()

    for j in range(NZ):

        @pl.when(zl != j)
        def _():
            tile_wait(0, j)

    for d in range(1, NY):
        t_y(0, d).start()
    v_step(1, 0)

    @pl.when(zh == 0)
    def _():
        pl.semaphore_wait(in_far, 9)
        for d in range(NX):
            label_far(d).start()
        for j in range(NZ):
            tile_far(j).start()

    for d in range(NX):
        rc(lx.at[0, 0], lx.at[1, d], lfs.at[d], lxr.at[1, d], dev(hh=1 - zh, xx=xat(d))).wait_recv()
    ly[1, y] = (lx[1, 0] + lx[1, 1]) + (lx[1, 2] + lx[1, 3])
    for d in range(1, NY):
        label_y(1, d).start()
    for j in range(NZ):
        tile_wait(1, j)
    for d in range(1, NY):
        t_y(1, d).start()
    v_step(2, 0)
    for d in range(1, NY):
        t_y_wait(0, d)
    relayout(0)
    t_x_start(0)
    for d in range(1, NY):
        label_y_wait(1, d)
    compact(1)
    v_step(3, 0)
    for d in range(1, NY):
        t_y_wait(1, d)
    relayout(1)
    t_x_start(1)
    v_step(1, 1)
    t_x_relay(0)
    v_step(4, 0)
    v_step(2, 1)
    t_x_relay(1)
    v_step(5, 0)
    v_step(3, 1)
    v_step(4, 1)
    t_x_end(0)
    t_x_end(1)

    multiply(zl, first=True)

    @pl.loop(1, NZ - 1)
    def _(k):
        multiply_at(k)

    for sub in range(NS):
        multiply_last(0, sub)

    def swap(sub):
        here = pl.ds(sub * ROWS, ROWS)
        return rc(xs.at[here], xr.at[here], cs.at[0, sub], cs.at[1, sub], dev(cc=1 - c))

    def put(sub):
        here = pl.ds(sub * ROWS, ROWS)
        return pltpu.make_async_copy(out.at[here], out_hbm.at[here], outs.at[sub])

    for sub in range(NS):
        v_arrive(NZ - 1, 1, sub)
        multiply_last(1, sub)
        here = pl.ds(sub * ROWS, ROWS)
        xs[here, :] = jnp.where(c == 0, acc[here, 256:], acc[here, :256]).astype(BF16)
        swap(sub).start()
    for sub in range(NS):
        here = pl.ds(sub * ROWS, ROWS)
        own = jnp.where(c == 0, acc[here, :256], acc[here, 256:]) + res[here, :].astype(F32)
        swap(sub).wait_recv()
        out[here, :] = ((own + xr[here, :].astype(F32)) / den[here, :]).astype(BF16)
        put(sub).start()

    for d in range(1, NX):
        label_x(d).wait_send()
    for d in range(NX):
        label_far(d).wait_send()
    for j in range(NZ):

        @pl.when(zl != j)
        def _():
            tile_near(j).wait_send()

        tile_far(j).wait_send()
    for hi in range(2):
        for d in range(1, NY):
            label_y(hi, d).wait_send()
            t_y(hi, d).wait_send()
        for way in range(2):
            t_x(hi, way, 0).wait_send()
            t_x(hi, way, 1).wait_send()
            t_x_on(hi, way).wait_send()
        for sub in range(NS):
            for way in range(2):
                for k in range(NZ - 1):

                    @pl.when(v_goes(way, k))
                    def _():
                        v_out(way, k, hi, sub).wait_send()

    for sub in range(NS):
        swap(sub).wait_send()
        put(sub).wait()


def local(integrals, amplitudes, cd_irrep, residual, ab_energy, ij_energy):
    anywhere = pl.BlockSpec(memory_space=pl.ANY)
    dma = pltpu.SemaphoreType.DMA
    return pl.pallas_call(
        kernel,
        out_shape=jax.ShapeDtypeStruct((512, 256), BF16),
        in_specs=[anywhere] * 6,
        out_specs=anywhere,
        scratch_shapes=[
            pltpu.SMEM((1, 16), jnp.int32),
            pltpu.VMEM((16, 3072), BF16),
            pltpu.VMEM((512, 1024), BF16),
            pltpu.VMEM((512, 256), BF16),
            pltpu.VMEM((1, 512), F32),
            pltpu.VMEM((1, 256), F32),
            pltpu.VMEM((512, 256), F32),
            pltpu.VMEM((2, NX, 1, 128), F32),
            pltpu.VMEM((2, NY, 1, 128), F32),
            pltpu.VMEM((NZ, 16, 128), BF16),
            pltpu.VMEM((2, NY, NZ, 16, 128), BF16),
            pltpu.VMEM((2, NX, NZ, 32, 512), BF16),
            pltpu.VMEM((NZ, 2, NS, ROWS, 128), BF16),
            pltpu.VMEM((512, 512), F32),
            pltpu.VMEM((512, 256), BF16),
            pltpu.VMEM((512, 256), BF16),
            pltpu.VMEM((512, 256), BF16),
            dma((6,)),
            dma((NX - 1,)),
            dma((2, NX)),
            dma((NX,)),
            dma((2, NY - 1)),
            dma((2, NY - 1)),
            dma((2, NZ)),
            dma((2, NZ)),
            dma((2, NY - 1)),
            dma((2, NY - 1)),
            dma((2, 2, 3)),
            dma((2, 2, 3)),
            dma((2, NZ - 1, 2, NS)),
            dma((2, NZ - 1, 2, NS)),
            dma((2, NS)),
            dma((NS,)),
            pltpu.SemaphoreType.REGULAR,
            pltpu.SemaphoreType.REGULAR,
        ],
        compiler_params=pltpu.CompilerParams(
            collective_id=0, has_side_effects=True, vmem_limit_bytes=56 * 1024 * 1024
        ),
        cost_estimate=pl.CostEstimate(flops=2 * 512 * 1536 * 512, bytes_accessed=2 << 20, transcendentals=0),
    )(
        integrals.reshape(512, 1024),
        amplitudes.reshape(16, 3072),
        cd_irrep,
        residual,
        ab_energy.reshape(1, 512),
        ij_energy.reshape(1, 256),
    )


def solution(mesh):
    return jax.shard_map(
        local,
        mesh=mesh,
        in_specs=(
            P("ab", "cd", None),
            P("cd", "ab", None),
            P("cd", "ab"),
            P("ab", "cd"),
            P("ab"),
            P("cd"),
        ),
        out_specs=P("ab", "cd"),
        check_vma=False,
    )
```
